512 devices in a mesh: fsdp: 32 (over z, core), tensor: 16 (over y, x).
Axes of the slice: x: 4, y: 4, z: 16, core: 2. Of those that a mesh axis runs over, the one named last changes fastest.
Arguments:
- hidden: bfloat16 [4096, 14336], P('fsdp', 'tensor'), may hold values from -6 to 6
- grad_out: bfloat16 [4096, 4096], P('fsdp', 'tensor'), may hold values from -6 to 6
- weight_slots: bfloat16 [16, 512, 4096], P('tensor', 'fsdp'), may hold values from -0.09375 to 0.09375
- block_ids: int32 [16, 512], P('tensor', 'fsdp'), may hold values from 0 to 895, as said below
- slot_count: int32 [16, 32], P('tensor', 'fsdp'), may hold values from 2 to 16, as said below
Outputs:
- projected: bfloat16 [4096, 4096], P('fsdp', 'tensor')
- d_hidden: bfloat16 [4096, 14336], P('fsdp', 'tensor')
- grad_slots: float32 [16, 512, 4096], P('tensor', 'fsdp')
The draws below stay inside these ranges and needn't reach their ends.
Inputs may be any that keep to these rules, and one draw needn't show every extreme that they name: `block_ids`: entry k of tensor shard s names the block at block row r and block column c of that shard's 14 x 64 grid as r * 64 + c; the 512 entries of one shard are all distinct; entries j * 16 to j * 16 + 15 are the slots stored by fsdp index j. The first slot_count[s, j] slots of fsdp index j in tensor shard s hold kept blocks; its other slots are empty.
All inputs are finite; a program needn't handle non-finite values.
Results may differ from the reference program's by a relative error of at most 0.018.
Values may be sent and summed in bfloat16 or wider, within the bound.
A program may use at most 128 MiB of HBM per device.

```python
import math
import jax
import jax.numpy as jnp
from jax import lax

D = 4096
FF = 14336
BLK = 64
TOK_DEV = 128
CAP = 16
TOKENS = 4096
ROWS_DEV = 896
BROWS = 14
BCOLS = 64
SLOTS = 512
N_FSDP = 32
N_TENSOR = 16


def draw_slot_count(key, part):
    key = jax.random.fold_in(key, 11)
    keys = jax.random.split(key, 4)
    levels = jax.random.randint(keys[0], (N_TENSOR, 1), CAP // 2, CAP + 1)
    drops = jax.random.randint(keys[1], (N_TENSOR, N_FSDP), 0, CAP // 4 + 1)
    counts = jnp.maximum(levels - drops, 2)
    full_shard = jax.random.randint(keys[2], (), 0, N_TENSOR)
    full_owner = jax.random.randint(keys[3], (), 0, N_FSDP)
    shard_grid = jnp.arange(N_TENSOR)[:, None]
    owner_grid = jnp.arange(N_FSDP)[None, :]
    chosen = (shard_grid == full_shard) & (owner_grid == full_owner)
    lowest = (shard_grid == (full_shard + 1) % N_TENSOR) & (owner_grid == full_owner)
    counts = jnp.where(lowest, 2, counts)
    return jnp.where(chosen, CAP, counts).astype(jnp.int32)


def draw_block_ids(key, part):
    key = jax.random.fold_in(key, 23)
    total_blocks = BROWS * BCOLS
    shard_keys = jax.random.split(key, N_TENSOR)

    def one_shard(shard_key):
        perm_key, owner_key = jax.random.split(shard_key)
        middle = (jax.random.permutation(perm_key, total_blocks - 2) + 1).astype(jnp.int32)
        ends = jnp.array([total_blocks - 1, 0], jnp.int32)
        ordered = jnp.concatenate([ends, middle])[:SLOTS]
        owner_index = jax.random.randint(owner_key, (), 0, N_FSDP)
        return jnp.roll(ordered, owner_index * CAP)
    return jax.vmap(one_shard)(shard_keys).astype(jnp.int32)


def block_levels(own_key, dims, shards, smallest, high):
    def one(dim, parts):
        heights = jax.random.uniform(jax.random.fold_in(jax.random.fold_in(own_key, 6), dim), (parts,), jnp.float32, smallest / len(shards), high / len(shards))
        return jnp.repeat(jnp.exp(heights), dims[dim] // parts).reshape((-1,) + (1,) * (len(dims) - dim - 1))

    factor_of = one(*shards[0])
    for cut in shards[1:]:
        factor_of = factor_of * one(*cut)
    return factor_of


def gaussian(own_key, shape, deviation, reach, cuts=(), held_as=jnp.bfloat16):
    values = deviation * jax.random.normal(own_key, shape, jnp.float32)
    if cuts:
        values = values * block_levels(own_key, shape, cuts, -0.22, 0.18)
    return jnp.clip(values, -reach, reach).astype(held_as)


def setup_inputs(seed: int = 0) -> dict:
    splits = jax.random.split(jax.random.key(seed), 6)
    return {
        "hidden": gaussian(splits[0], (TOKENS, FF), 1.0, 6.0, ((0, 32), (1, 16))),
        "grad_out": gaussian(splits[1], (TOKENS, D), 1.0, 6.0, ((0, 32), (1, 16))),
        "weight_slots": gaussian(splits[2], (N_TENSOR, SLOTS, BLK * BLK), (FF // 3) ** -0.5, 0.09375, ((0, 16), (1, 32))),
        "block_ids": draw_block_ids(jax.random.fold_in(splits[5], 71), 0),
        "slot_count": draw_slot_count(jax.random.fold_in(splits[5], 71), 0),
    }


def build_window(slot_blocks, block_index, stored_counts):
    live_slots = jnp.arange(SLOTS) % CAP < jnp.repeat(stored_counts, CAP, total_repeat_length=SLOTS)
    kept_blocks = jnp.where(live_slots[:, None], slot_blocks, jnp.zeros_like(slot_blocks))
    block_grid = jnp.zeros((BROWS * BCOLS, BLK * BLK), slot_blocks.dtype).at[block_index].set(kept_blocks)
    block_grid = block_grid.reshape(BROWS, BCOLS, BLK, BLK).transpose(0, 2, 1, 3)
    return (block_grid.reshape(ROWS_DEV, D), live_slots)

def reference(hidden, grad_out, weight_slots, block_ids, slot_count):
    grad_scale = 1.0 / math.sqrt(TOKENS)

    def shard_step(running, inputs):
        shard_index, slot_blocks, block_index, stored_counts = inputs
        window_dense, live_slots = build_window(slot_blocks, block_index, stored_counts)
        local_hidden = lax.dynamic_slice_in_dim(hidden, (shard_index * ROWS_DEV).astype(jnp.int32), ROWS_DEV, 1)
        partial_value = jnp.dot(local_hidden, window_dense, preferred_element_type=jnp.float32)
        running = running + partial_value.astype(jnp.bfloat16).astype(jnp.float32)
        d_local = jnp.dot(grad_out, window_dense.T, preferred_element_type=jnp.float32).astype(jnp.bfloat16)
        row_index = block_index // BCOLS
        col_index = block_index % BCOLS

        def group_step(accum, group_index):
            first_token = (group_index * TOK_DEV).astype(jnp.int32)
            hidden_group = lax.dynamic_slice_in_dim(local_hidden, first_token, TOK_DEV, 0)
            grad_group = lax.dynamic_slice_in_dim(grad_out, first_token, TOK_DEV, 0)
            group_product = jnp.dot(hidden_group.T, grad_group, preferred_element_type=jnp.float32).astype(jnp.bfloat16)
            picked = group_product.reshape(BROWS, BLK, BCOLS, BLK)[row_index, :, col_index, :]
            return (accum + picked.reshape(SLOTS, BLK * BLK).astype(jnp.float32), None)
        accum, unused = lax.scan(group_step, jnp.zeros((SLOTS, BLK * BLK), jnp.float32), jnp.arange(N_FSDP, dtype=jnp.int32))
        grad_blocks = jnp.where(live_slots[:, None], accum * grad_scale, jnp.zeros_like(accum))
        return (running, (d_local, grad_blocks))
    start_sum = jnp.zeros((TOKENS, D), jnp.float32)
    shard_numbers = jnp.arange(N_TENSOR, dtype=jnp.int32)
    running, (d_parts, grad_slots) = lax.scan(shard_step, start_sum, (shard_numbers, weight_slots, block_ids, slot_count))
    projected = running.astype(jnp.bfloat16)
    d_hidden = d_parts.transpose(1, 0, 2).reshape(TOKENS, FF)
    return (projected, d_hidden, grad_slots)
```

```python
import functools
import math

import jax
import jax.numpy as jnp
from jax import lax
from jax.experimental import pallas as pl
from jax.experimental.pallas import tpu as pltpu
from jax.sharding import PartitionSpec as P

BLK = 64
HALF = BLK // 2
LANES = 2 * BLK
MESH = pl.DeviceIdType.MESH
F32 = jnp.float32
BF16 = jnp.bfloat16
NN = (((1,), (0,)), ((), ()))
NT = (((1,), (1,)), ((), ()))


def dot(a, b, dims=NN):
    return lax.dot_general(a, b, dims, preferred_element_type=F32)


def lane_iota(shape):
    return lax.broadcasted_iota(jnp.int32, shape, 1)


def kernel(
    n_f, n_t,
    hid_ref, grad_ref, w_ref, ids_ref,
    proj_ref, dh_ref, gs_ref,
    wall, ids_all, fg, h2, hm, gd, q, bw,
    g_own, g_oth, g_sib, ring_r, ring_l, send_r, send_l,
    parts, psend, dacc, inv_v, ids_v, inv_s, ids_s,
    ids_ss, ids_rs, gr_ss, gr_rs, wr_ss, wr_rs, wl_ss, wl_rs, wb_ss, wb_rs,
    gs_ss, gs_rs, rr_ss, rr_rs, rl_ss, rl_rs, pp_ss, pp_rs, loc_s,
):
    cap = w_ref.shape[0]
    half = cap // 2
    toks, units = hid_ref.shape
    cols = grad_ref.shape[1]
    brows = units // BLK
    rows = units // 2
    bcols = n_t * cols // BLK
    n_z = n_f // 2
    h = n_z // 2
    empty = n_f * cap

    f = lax.axis_index("fsdp")
    t = lax.axis_index("tensor")
    z, c = f // 2, f % 2

    def chip(offset):
        return lax.rem(z + offset + n_z, n_z)

    right, left, sib = chip(1) * 2 + c, chip(-1) * 2 + c, z * 2 + 1 - c

    def fpeer(i):
        return lax.rem(f + i, n_f)

    def tpeer(i):
        return lax.rem(t + i, n_t)

    def to_f(src, dst, ss, rs, peer):
        return pltpu.make_async_remote_copy(
            src_ref=src, dst_ref=dst, send_sem=ss, recv_sem=rs,
            device_id={"fsdp": peer}, device_id_type=MESH,
        )

    def to_t(src, dst, ss, rs, peer):
        return pltpu.make_async_remote_copy(
            src_ref=src, dst_ref=dst, send_sem=ss, recv_sem=rs,
            device_id={"tensor": peer}, device_id_type=MESH,
        )

    barrier = pltpu.get_barrier_semaphore()

    def greet_f(i, carry):
        pl.semaphore_signal(barrier, inc=1, device_id={"fsdp": fpeer(i)}, device_id_type=MESH)
        return carry

    def greet_t(i, carry):
        pl.semaphore_signal(barrier, inc=1, device_id={"tensor": tpeer(i)}, device_id_type=MESH)
        return carry

    lax.fori_loop(1, n_f, greet_f, 0)
    lax.fori_loop(1, n_t, greet_t, 0)
    pl.semaphore_wait(barrier, n_f + n_t - 2)

    def w_part(zz, cc, lo, size):
        return wall.at[pl.ds((zz * 2 + cc) * cap + lo, size)]

    def w_right(s):
        src = w_ref if s == 0 else w_part(chip(-s), c, 0, cap)
        dst = w_part(chip(-s), c, 0, cap)
        if s == h - 1:
            src = (w_ref if s == 0 else w_part(chip(-s), c, 0, cap)).at[pl.ds(0, half)]
            dst = w_part(chip(-s), c, 0, half)
        return to_f(src, dst, wr_ss.at[s], wr_rs.at[s], right)

    def w_left(s):
        src = w_ref if s == 0 else w_part(chip(s), c, 0, cap)
        dst = w_part(chip(s), c, 0, cap)
        if s == h - 1:
            src = src.at[pl.ds(half, half)]
            dst = w_part(chip(s), c, half, half)
        return to_f(src, dst, wl_ss.at[s], wl_rs.at[s], left)

    def w_arrived_right(a):
        size = half if a == h - 1 else cap
        ref = w_part(chip(-1 - a), c, 0, size)
        return to_f(ref, ref, wr_ss.at[a], wr_rs.at[a], right)

    def w_arrived_left(a):
        lo, size = (half, half) if a == h - 1 else (0, cap)
        ref = w_part(chip(1 + a), c, lo, size)
        return to_f(ref, ref, wl_ss.at[a], wl_rs.at[a], left)

    def w_sib(k, core):
        if k == 0:
            src = w_ref if core is c else w_part(z, core, 0, cap)
            dst = w_part(z, core, 0, cap)
        elif k <= h:
            a = k - 1
            src = dst = w_part(chip(-1 - a), core, 0, half if a == h - 1 else cap)
        else:
            a = k - 1 - h
            lo, size = (half, half) if a == h - 1 else (0, cap)
            src = dst = w_part(chip(1 + a), core, lo, size)
        return to_f(src, dst, wb_ss.at[k], wb_rs.at[k], sib)

    def ids_copy(i):
        return to_f(ids_ref, ids_all.at[f], ids_ss.at[i], ids_rs.at[f], fpeer(i))

    def ids_arrival(i):
        peer = fpeer(i)
        return to_f(ids_all.at[peer], ids_all.at[peer], ids_ss.at[i], ids_rs.at[peer], peer)

    def grad_copy(i):
        return to_t(grad_ref, fg.at[t], gr_ss.at[i], gr_rs.at[t], tpeer(i))

    def grad_arrival(i):
        peer = tpeer(i)
        return to_t(fg.at[peer], fg.at[peer], gr_ss.at[i], gr_rs.at[peer], peer)

    w_right(0).start()
    w_left(0).start()
    w_sib(0, c).start()

    def start_ids(i, carry):
        ids_copy(i).start()
        return carry

    def start_grad(i, carry):
        grad_copy(i).start()
        return carry

    lax.fori_loop(1, n_f, start_ids, 0)
    lax.fori_loop(1, n_t, start_grad, 0)

    wall[pl.ds(f * cap, cap)] = w_ref[...]
    wall[pl.ds(empty, 8)] = jnp.zeros((8, HALF, LANES), BF16)
    ids_all[f] = ids_ref[...]
    fg[t] = grad_ref[...]

    def pick_units(odd, shape, unit_axis):
        unit = lax.broadcasted_iota(jnp.int32, shape, unit_axis)
        out = lax.broadcasted_iota(jnp.int32, shape, 1 - unit_axis)
        return jnp.where(unit == 2 * out + odd, 1.0, 0.0).astype(BF16)

    def split_hidden():
        for lo in range(0, units, 256):
            size = min(256, units - lo)
            chunk = hid_ref[:, lo:lo + size]
            for odd in range(2):
                sel = pick_units(odd, (size // 2, size), 1)
                h2[lo // 2:(lo + size) // 2, odd * toks:(odd + 1) * toks] = dot(sel, chunk, NT).astype(BF16)
                hm[odd * toks:(odd + 1) * toks, lo // 2:(lo + size) // 2] = dot(chunk, sel, NT).astype(BF16)

    def positions():
        def wait_ids(i, carry):
            ids_arrival(i).wait_recv()
            return carry

        lax.fori_loop(1, n_f, wait_ids, 0)
        lane = lane_iota((cap, LANES))
        row = lax.broadcasted_iota(jnp.int32, (cap, LANES), 0)
        groups = -(-brows * bcols // LANES)

        def owner(j, accs):
            x = ids_all[j]
            ids_v[pl.ds(j, 1), :] = jnp.sum(jnp.where(row == lane, x, 0), axis=0, keepdims=True)
            slot = row + j * cap
            return tuple(
                jnp.minimum(acc, jnp.where(x == lane + p * LANES, slot, empty))
                for p, acc in enumerate(accs)
            )

        accs = lax.fori_loop(
            0, n_f, owner, tuple(jnp.full((cap, LANES), empty, jnp.int32) for _ in range(groups))
        )
        for p, acc in enumerate(accs):
            inv_v[p:p + 1, :] = jnp.min(acc, axis=0, keepdims=True)
        one = pltpu.make_async_copy(inv_v, inv_s, loc_s.at[0])
        two = pltpu.make_async_copy(ids_v, ids_s, loc_s.at[1])
        one.start()
        two.start()
        one.wait()
        two.wait()

    def product(u, carry):
        src = fg[u // 2, :, pl.ds(pl.multiple_of(lax.rem(u, 2) * LANES, LANES), LANES)].astype(F32)
        swapped = pltpu.roll(src, BLK, 1)
        low = lane_iota((toks, LANES)) < BLK
        gd[u, 0:toks, 0:LANES] = jnp.where(low, src, 0.0).astype(BF16)
        gd[u, toks:2 * toks, 0:LANES] = jnp.where(low, 0.0, swapped).astype(BF16)
        gd[u, 0:toks, LANES:2 * LANES] = jnp.where(low, swapped, 0.0).astype(BF16)
        gd[u, toks:2 * toks, LANES:2 * LANES] = jnp.where(low, 0.0, src).astype(BF16)
        res = dot(h2[...], gd[u]).astype(BF16)
        for r in range(brows):
            q[r * bcols + 2 * u] = res[r * HALF:(r + 1) * HALF, 0:LANES]
            q[r * bcols + 2 * u + 1] = res[r * HALF:(r + 1) * HALF, LANES:2 * LANES]
        return carry

    def wait_grads():
        def wait_grad(i, carry):
            grad_arrival(i).wait_recv()
            return carry

        lax.fori_loop(1, n_t, wait_grad, 0)

    n_u = 2 * n_t
    for a in range(h):
        w_arrived_right(a).wait_recv()
        if a < h - 1:
            w_right(a + 1).start()
        w_sib(1 + a, c).start()
        w_arrived_left(a).wait_recv()
        if a < h - 1:
            w_left(a + 1).start()
        w_sib(1 + h + a, c).start()
        if a == 0:
            split_hidden()
        if a == min(1, h - 1):
            positions()
        if a == min(3, h - 1):
            wait_grads()
        if h == 8:
            if 3 <= a <= 6:
                lax.fori_loop((a - 3) * n_u // 4, (a - 2) * n_u // 4, product, 0)
        elif a == h - 1:
            lax.fori_loop(0, n_u, product, 0)

    def pick(d):
        def one(i, carry):
            g_own[d, i] = q[ids_s[2 * d + c, i]]
            g_oth[d, i] = q[ids_s[2 * d + 1 - c, i]]
            return carry

        lax.fori_loop(0, cap, one, 0, unroll=4)
        g_copy(d).start()

    def g_copy(d):
        return to_f(g_oth.at[d], g_sib.at[d], gs_ss.at[d], gs_rs.at[d], sib)

    def total(d, lo, size, arrived=None):
        part = pl.ds(lo, size)
        value = g_own[d, part].astype(F32) + g_sib[d, part].astype(F32)
        return value if arrived is None else value + arrived.astype(F32)

    def ring_copy(s, buf, dst, ss, rs, peer, lo):
        part = pl.ds(lo, half if s == 0 else cap)
        return to_f(buf.at[s, part], dst.at[s, part], ss.at[s], rs.at[s], peer)

    def right_copy(s):
        return ring_copy(s, send_r, ring_r, rr_ss, rr_rs, right, 0)

    def left_copy(s):
        return ring_copy(s, send_l, ring_l, rl_ss, rl_rs, left, half if s == 0 else 0)

    def combine(s):
        d = chip(h - s)
        g_copy(d).wait_recv()
        if s == 0:
            send_r[0, 0:half] = total(d, 0, half).astype(BF16)
            right_copy(0).start()
            send_l[0, half:cap] = total(d, half, half).astype(BF16)
            left_copy(0).start()
            return
        right_copy(s - 1).wait_recv()
        if s == 1:
            send_r[1, 0:half] = total(d, 0, half, ring_r[0, 0:half]).astype(BF16)
            send_r[1, half:cap] = total(d, half, half).astype(BF16)
        else:
            send_r[s] = total(d, 0, cap, ring_r[s - 1]).astype(BF16)
        right_copy(s).start()
        d = chip(s - h)
        g_copy(d).wait_recv()
        left_copy(s - 1).wait_recv()
        if s == 1:
            send_l[1, 0:half] = total(d, 0, half).astype(BF16)
            send_l[1, half:cap] = total(d, half, half, ring_l[0, half:cap]).astype(BF16)
        else:
            send_l[s] = total(d, 0, cap, ring_l[s - 1]).astype(BF16)
        left_copy(s).start()

    def part_copy(peer):
        return to_t(psend.at[peer], parts.at[t], pp_ss.at[peer], pp_rs.at[t], peer)

    def columns(i, carry):
        tt = tpeer(i)
        low = lane_iota((toks, LANES)) < BLK
        for v in range(2):
            u = tt * 2 + v
            for r in range(brows):
                for side in range(2):
                    pos = r * bcols + 2 * u + side
                    bw[v, r * HALF:(r + 1) * HALF, side * LANES:(side + 1) * LANES] = wall[
                        inv_s[lax.div(pos, LANES), lax.rem(pos, LANES)]
                    ]
            res = dot(hm[...], bw[v])
            top_a, top_b = res[0:toks, 0:LANES], res[0:toks, LANES:2 * LANES]
            bot_a, bot_b = res[toks:2 * toks, 0:LANES], res[toks:2 * toks, LANES:2 * LANES]
            tile = jnp.where(low, top_a, bot_b) + pltpu.roll(jnp.where(low, top_b, bot_a), BLK, 1)
            psend[tt, :, v * LANES:(v + 1) * LANES] = tile.astype(BF16)
            dacc[...] += dot(gd[u], bw[v], NT)
        return carry

    def columns_and_send(i, carry):
        columns(i, carry)
        part_copy(tpeer(i)).start()
        return carry

    dacc[...] = jnp.zeros_like(dacc)
    pick(chip(h))
    if h > 1:
        pick(chip(h - 1))
        pick(chip(1 - h))
    combine(0)
    for k in range(2 * h + 1):
        w_sib(k, 1 - c).wait_recv()

    for s in range(h):
        if s > 0:
            combine(s)
        if s + 2 < h:
            pick(chip(h - s - 2))
            pick(chip(s + 2 - h))
        elif s + 2 == h or h == 1:
            pick(chip(0))
        lo, hi = s * n_t // h, (s + 1) * n_t // h
        if s == h - 1:
            lax.fori_loop(1 + lo, hi, columns_and_send, 0)
            columns(0, 0)
        else:
            lax.fori_loop(1 + lo, 1 + hi, columns_and_send, 0)

    for lo in range(0, units, 256):
        size = min(256, units - lo)
        even = dacc[0:toks, lo // 2:(lo + size) // 2].astype(BF16)
        odd = dacc[toks:2 * toks, lo // 2:(lo + size) // 2].astype(BF16)
        dh_ref[:, lo:lo + size] = (
            dot(even, pick_units(0, (size // 2, size), 1))
            + dot(odd, pick_units(1, (size // 2, size), 1))
        ).astype(BF16)

    proj_acc = psend[t].astype(F32)
    for i in range(1, n_t):
        peer = tpeer(i)
        to_t(parts.at[peer], parts.at[peer], pp_ss.at[peer], pp_rs.at[peer], peer).wait_recv()
        proj_acc += parts[peer].astype(F32)
    proj_ref[...] = proj_acc.astype(BF16)

    g_copy(z).wait_recv()
    right_copy(h - 1).wait_recv()
    left_copy(h - 1).wait_recv()
    gs_ref[...] = total(z, 0, cap) + ring_r[h - 1].astype(F32) + ring_l[h - 1].astype(F32)

    def sent_f(i, carry):
        ids_copy(i).wait_send()
        return carry

    def sent_t(i, carry):
        grad_copy(i).wait_send()
        part_copy(tpeer(i)).wait_send()
        return carry

    lax.fori_loop(1, n_f, sent_f, 0)
    lax.fori_loop(1, n_t, sent_t, 0)
    for s in range(h):
        w_right(s).wait_send()
        w_left(s).wait_send()
        right_copy(s).wait_send()
        left_copy(s).wait_send()
    for k in range(2 * h + 1):
        w_sib(k, c).wait_send()

    def sent_g(d, carry):
        g_copy(d).wait_send()
        return carry

    lax.fori_loop(0, n_z, sent_g, 0)


def on_device(hidden, grad_out, weight_slots, block_ids, slot_count):
    n_f, n_t = lax.axis_size("fsdp"), lax.axis_size("tensor")
    toks, units = hidden.shape
    cols = grad_out.shape[1]
    cap = weight_slots.shape[1]
    n_z = n_f // 2
    h = n_z // 2
    brows, bcols = units // BLK, n_t * cols // BLK
    live = jnp.arange(cap) < slot_count[0, 0]
    packed = jnp.where(live[:, None], weight_slots[0], 0).reshape(cap, HALF, LANES)
    ids = jnp.broadcast_to(block_ids[0][:, None], (cap, LANES))
    block = (cap, HALF, LANES)
    dma = pltpu.SemaphoreType.DMA
    vmem = pl.BlockSpec(memory_space=pltpu.VMEM)
    groups = -(-brows * bcols // LANES)
    projected, d_hidden, grads = pl.pallas_call(
        functools.partial(kernel, n_f, n_t),
        out_shape=(
            jax.ShapeDtypeStruct((toks, cols), BF16),
            jax.ShapeDtypeStruct((toks, units), BF16),
            jax.ShapeDtypeStruct(block, F32),
        ),
        in_specs=[vmem] * 4,
        out_specs=(vmem, vmem, vmem),
        scratch_shapes=[
            pltpu.VMEM((n_f * cap + 8, HALF, LANES), BF16),
            pltpu.VMEM((n_f, cap, LANES), jnp.int32),
            pltpu.VMEM((n_t, toks, cols), BF16),
            pltpu.VMEM((units // 2, 2 * toks), BF16),
            pltpu.VMEM((2 * toks, units // 2), BF16),
            pltpu.VMEM((2 * n_t, 2 * toks, 2 * LANES), BF16),
            pltpu.VMEM((brows * bcols, HALF, LANES), BF16),
            pltpu.VMEM((2, units // 2, 2 * LANES), BF16),
            pltpu.VMEM((n_z,) + block, BF16),
            pltpu.VMEM((n_z,) + block, BF16),
            pltpu.VMEM((n_z,) + block, BF16),
            pltpu.VMEM((h,) + block, BF16),
            pltpu.VMEM((h,) + block, BF16),
            pltpu.VMEM((h,) + block, BF16),
            pltpu.VMEM((h,) + block, BF16),
            pltpu.VMEM((n_t, toks, cols), BF16),
            pltpu.VMEM((n_t, toks, cols), BF16),
            pltpu.VMEM((2 * toks, units // 2), F32),
            pltpu.VMEM((groups, LANES), jnp.int32),
            pltpu.VMEM((n_f, LANES), jnp.int32),
            pltpu.SMEM((groups, LANES), jnp.int32),
            pltpu.SMEM((n_f, LANES), jnp.int32),
            dma((n_f,)), dma((n_f,)), dma((n_t,)), dma((n_t,)),
            dma((h,)), dma((h,)), dma((h,)), dma((h,)),
            dma((2 * h + 1,)), dma((2 * h + 1,)),
            dma((n_z,)), dma((n_z,)),
            dma((h,)), dma((h,)), dma((h,)), dma((h,)),
            dma((n_t,)), dma((n_t,)), dma((2,)),
        ],
        compiler_params=pltpu.CompilerParams(
            collective_id=0, has_side_effects=True, vmem_limit_bytes=56 * 1024 * 1024
        ),
        cost_estimate=pl.CostEstimate(
            flops=10 * toks * units * n_t * cols, bytes_accessed=2 * 1024 * 1024, transcendentals=0
        ),
    )(hidden, grad_out, packed, ids)
    scale = 1.0 / math.sqrt(toks * n_f)
    flat = grads.reshape(cap, BLK * BLK)
    grad_blocks = jnp.where(live[:, None], flat * scale, jnp.zeros_like(flat))
    return (projected, d_hidden, grad_blocks[None])


def solution(mesh):
    in_specs = (
        P("fsdp", "tensor"),
        P("fsdp", "tensor"),
        P("tensor", "fsdp", None),
        P("tensor", "fsdp"),
        P("tensor", "fsdp"),
    )
    out_specs = (P("fsdp", "tensor"), P("fsdp", "tensor"), P("tensor", "fsdp", None))
    return jax.shard_map(
        on_device, mesh=mesh, in_specs=in_specs, out_specs=out_specs, check_vma=False
    )
```

```python
import functools
import math

import jax
import jax.numpy as jnp
from jax import lax
from jax.experimental import pallas as pl
from jax.experimental.pallas import tpu as pltpu
from jax.sharding import PartitionSpec as P

BLK = 64
HALF = BLK // 2
LANES = 2 * BLK
MESH = pl.DeviceIdType.MESH
F32 = jnp.float32
BF16 = jnp.bfloat16
K = 2
NN = (((1,), (0,)), ((), ()))
NT = (((1,), (1,)), ((), ()))


def dot(a, b, dims=NN):
    return lax.dot_general(a, b, dims, preferred_element_type=F32)


def lane_iota(shape):
    return lax.broadcasted_iota(jnp.int32, shape, 1)


def kernel(
    n_f, n_t,
    hid_ref, grad_ref, slots_ref, ids_ref, count_ref,
    proj_ref, dh_ref, gs_ref,
    wall, flat, w_ref, ids_all, fg, h2, hm, gd, q, bw,
    g_own, g_oth, g_sib, ring_r, ring_l, send_r, send_l,
    parts, psend, dacc, inv_v, inv_s, ids_s,
    ids_ss, ids_rs, gr_ss, gr_rs, wr_ss, wr_rs, wl_ss, wl_rs, wb_ss, wb_rs,
    gs_ss, gs_rs, rr_ss, rr_rs, rl_ss, rl_rs, pp_ss, pp_rs, loc_s,
):
    cap = slots_ref.shape[1]
    half, step = cap // 2, cap // K
    toks, units = hid_ref.shape
    cols = grad_ref.shape[1]
    brows = units // BLK
    rows = units // 2
    bcols = n_t * cols // BLK
    n_z = n_f // 2
    h = n_z // 2
    empty = n_f * cap

    f = lax.axis_index("fsdp")
    t = lax.axis_index("tensor")
    z, c = f // 2, f % 2

    def chip(offset):
        return lax.rem(z + offset + n_z, n_z)

    right, left, sib = chip(1) * 2 + c, chip(-1) * 2 + c, z * 2 + 1 - c

    def fpeer(i):
        return lax.rem(f + i, n_f)

    def tpeer(i):
        return lax.rem(t + i, n_t)

    def to_f(src, dst, ss, rs, peer):
        return pltpu.make_async_remote_copy(
            src_ref=src, dst_ref=dst, send_sem=ss, recv_sem=rs,
            device_id={"fsdp": peer}, device_id_type=MESH,
        )

    def to_t(src, dst, ss, rs, peer):
        return pltpu.make_async_remote_copy(
            src_ref=src, dst_ref=dst, send_sem=ss, recv_sem=rs,
            device_id={"tensor": peer}, device_id_type=MESH,
        )

    barrier = pltpu.get_barrier_semaphore()

    def greet_f(i, carry):
        pl.semaphore_signal(barrier, inc=1, device_id={"fsdp": fpeer(i)}, device_id_type=MESH)
        return carry

    def greet_t(i, carry):
        pl.semaphore_signal(barrier, inc=1, device_id={"tensor": tpeer(i)}, device_id_type=MESH)
        return carry

    lax.fori_loop(1, n_f, greet_f, 0)
    lax.fori_loop(1, n_t, greet_t, 0)
    live = lax.broadcasted_iota(jnp.int32, (cap, LANES), 0) < count_ref[0, 0]
    for i in range(HALF):
        piece = slots_ref[0, :, i * LANES:(i + 1) * LANES].astype(F32)
        flat[pl.ds(i, cap, stride=HALF), :] = jnp.where(live, piece, 0.0)
    w_ref[...] = flat[...].reshape(cap, HALF, LANES).astype(BF16)

    def w_part(zz, cc, lo, size):
        return wall.at[pl.ds((zz * 2 + cc) * cap + lo, size)]

    def w_right(s, j):
        dst = w_part(chip(-s), c, j * step, step)
        src = w_ref.at[pl.ds(j * step, step)] if s == 0 else dst
        return to_f(src, dst, wr_ss.at[s, j], wr_rs.at[s, j], right)

    def w_left(s, j):
        dst = w_part(chip(s), c, j * step, step)
        src = w_ref.at[pl.ds(j * step, step)] if s == 0 else dst
        return to_f(src, dst, wl_ss.at[s, j], wl_rs.at[s, j], left)

    def w_arrived_right(a, j):
        ref = w_part(chip(-1 - a), c, j * step, step)
        return to_f(ref, ref, wr_ss.at[a, j], wr_rs.at[a, j], right)

    def w_arrived_left(a, j):
        ref = w_part(chip(1 + a), c, j * step, step)
        return to_f(ref, ref, wl_ss.at[a, j], wl_rs.at[a, j], left)

    def w_sib(k, core):
        if k == 0:
            dst = w_part(z, core, 0, cap)
            src = w_ref if core is c else dst
        elif k <= h:
            a = k - 1
            src = dst = w_part(chip(-1 - a), core, 0, half if a == h - 1 else cap)
        else:
            a = k - 1 - h
            lo, size = (half, half) if a == h - 1 else (0, cap)
            src = dst = w_part(chip(1 + a), core, lo, size)
        return to_f(src, dst, wb_ss.at[k], wb_rs.at[k], sib)

    def ids_copy(i):
        return to_f(ids_ref, ids_all.at[pl.ds(f, 1)], ids_ss.at[i], ids_rs.at[f], fpeer(i))

    def ids_arrival(i):
        peer = fpeer(i)
        ref = ids_all.at[pl.ds(peer, 1)]
        return to_f(ref, ref, ids_ss.at[i], ids_rs.at[peer], peer)

    def grad_copy(i):
        return to_t(grad_ref, fg.at[t], gr_ss.at[i], gr_rs.at[t], tpeer(i))

    def grad_arrival(peer):
        return to_t(fg.at[peer], fg.at[peer], gr_ss.at[0], gr_rs.at[peer], peer)

    def chunks(s):
        return K // 2 if s == h - 1 else K

    def other(j):
        return (j + K // 2) % K

    def start_ids(i, carry):
        ids_copy(i).start()
        return carry

    def start_grad(i, carry):
        grad_copy(i).start()
        return carry

    pl.semaphore_wait(barrier, n_f + n_t - 2)
    lax.fori_loop(1, n_t, start_grad, 0)
    for j in range(chunks(0)):
        w_right(0, j).start()
        w_left(0, other(j)).start()
    w_sib(0, c).start()

    lax.fori_loop(1, n_f, start_ids, 0)

    wall[pl.ds(f * cap, cap)] = w_ref[...]
    wall[pl.ds(empty, 8)] = jnp.zeros((8, HALF, LANES), BF16)
    ids_all[pl.ds(f, 1), :] = ids_ref[...]
    fg[t] = grad_ref[...]

    def pick_units(odd, shape, unit_axis):
        unit = lax.broadcasted_iota(jnp.int32, shape, unit_axis)
        out = lax.broadcasted_iota(jnp.int32, shape, 1 - unit_axis)
        return jnp.where(unit == 2 * out + odd, 1.0, 0.0).astype(BF16)

    def split_hidden():
        for lo in range(0, units, 256):
            size = min(256, units - lo)
            chunk = hid_ref[:, lo:lo + size]
            for odd in range(2):
                sel = pick_units(odd, (size // 2, size), 1)
                h2[lo // 2:(lo + size) // 2, odd * toks:(odd + 1) * toks] = dot(sel, chunk, NT).astype(BF16)
                hm[odd * toks:(odd + 1) * toks, lo // 2:(lo + size) // 2] = dot(chunk, sel, NT).astype(BF16)

    def positions():
        def wait_ids(i, carry):
            ids_arrival(i).wait_recv()
            return carry

        lax.fori_loop(1, n_f, wait_ids, 0)
        lane = lane_iota((cap, LANES))
        diagonal = lane_iota((cap, cap)) == lax.broadcasted_iota(jnp.int32, (cap, cap), 0)
        row = lax.broadcasted_iota(jnp.int32, (cap, LANES), 0)
        groups = -(-brows * bcols // LANES)

        def owner(j, accs):
            x = jnp.sum(jnp.where(diagonal, ids_all[pl.ds(j, 1), :], 0), axis=1, keepdims=True)
            slot = row + j * cap
            return tuple(
                jnp.minimum(acc, jnp.where(x == lane + p * LANES, slot, empty))
                for p, acc in enumerate(accs)
            )

        accs = lax.fori_loop(
            0, n_f, owner, tuple(jnp.full((cap, LANES), empty, jnp.int32) for _ in range(groups))
        )
        for p, acc in enumerate(accs):
            inv_v[p:p + 1, :] = jnp.min(acc, axis=0, keepdims=True)
        one = pltpu.make_async_copy(inv_v, inv_s, loc_s.at[0])
        two = pltpu.make_async_copy(ids_all, ids_s, loc_s.at[1])
        one.start()
        two.start()
        one.wait()
        two.wait()

    def product(i, carry):
        tt = lax.rem(t - i + n_t, n_t)
        low = lane_iota((toks, LANES)) < BLK
        for v in range(2):
            u = 2 * tt + v
            src = fg[tt, :, v * LANES:(v + 1) * LANES].astype(F32)
            swapped = pltpu.roll(src, BLK, 1)
            gd[u, 0:toks, 0:LANES] = jnp.where(low, src, 0.0).astype(BF16)
            gd[u, toks:2 * toks, 0:LANES] = jnp.where(low, 0.0, swapped).astype(BF16)
            gd[u, 0:toks, LANES:2 * LANES] = jnp.where(low, swapped, 0.0).astype(BF16)
            gd[u, toks:2 * toks, LANES:2 * LANES] = jnp.where(low, 0.0, src).astype(BF16)
            res = dot(h2[...], gd[u]).astype(BF16)
            for r in range(brows):
                q[r * bcols + 2 * u] = res[r * HALF:(r + 1) * HALF, 0:LANES]
                q[r * bcols + 2 * u + 1] = res[r * HALF:(r + 1) * HALF, LANES:2 * LANES]
        return carry

    def products(lo, hi):
        if lo == 0 and hi > 0:
            product(0, 0)
            lo = 1

        def arrived(i, carry):
            grad_arrival(lax.rem(t - i + n_t, n_t)).wait_recv()
            return product(i, carry)

        if hi > lo:
            lax.fori_loop(lo, hi, arrived, 0)

    def pick(d):
        def one(i, carry):
            g_own[d, i] = q[ids_s[2 * d + c, i]]
            g_oth[d, i] = q[ids_s[2 * d + 1 - c, i]]
            return carry

        lax.fori_loop(0, cap, one, 0, unroll=4)
        g_copy(d).start()

    def g_copy(d):
        return to_f(g_oth.at[d], g_sib.at[d], gs_ss.at[d], gs_rs.at[d], sib)

    def right_copy(s, j):
        part = pl.ds(j * step, step)
        return to_f(send_r.at[s, part], ring_r.at[s, part], rr_ss.at[s, j], rr_rs.at[s, j], right)

    def left_copy(s, j):
        part = pl.ds(j * step, step)
        return to_f(send_l.at[s, part], ring_l.at[s, part], rl_ss.at[s, j], rl_rs.at[s, j], left)

    def wait_sums(s):
        for d in [chip(h - s)] if s in (0, h) else [chip(h - s), chip(s - h)]:
            g_copy(d).wait_recv()
            g_own[d] = g_own[d] + g_sib[d]

    def combine(s, j):
        arrives = s > 1 or (s == 1 and j < K // 2)
        part = pl.ds(j * step, step)
        if arrives:
            right_copy(s - 1, j).wait_recv()
        value = g_own[chip(h - s), part]
        send_r[s, part] = value + ring_r[s - 1, part] if arrives else value
        right_copy(s, j).start()
        j = other(j)
        part = pl.ds(j * step, step)
        if arrives:
            left_copy(s - 1, j).wait_recv()
        value = g_own[chip(s - h), part]
        send_l[s, part] = value + ring_l[s - 1, part] if arrives else value
        left_copy(s, j).start()

    def part_copy(peer):
        return to_t(psend.at[peer], parts.at[t], pp_ss.at[peer], pp_rs.at[t], peer)

    def part_arrival(peer):
        return to_t(parts.at[peer], parts.at[peer], pp_ss.at[peer], pp_rs.at[peer], peer)

    def columns(i, carry):
        tt = tpeer(i)
        low = lane_iota((toks, LANES)) < BLK
        for v in range(2):
            u = tt * 2 + v
            for r in range(brows):
                for side in range(2):
                    pos = r * bcols + 2 * u + side
                    bw[v, r * HALF:(r + 1) * HALF, side * LANES:(side + 1) * LANES] = wall[
                        inv_s[lax.div(pos, LANES), lax.rem(pos, LANES)]
                    ]
            res = dot(hm[...], bw[v])
            top_a, top_b = res[0:toks, 0:LANES], res[0:toks, LANES:2 * LANES]
            bot_a, bot_b = res[toks:2 * toks, 0:LANES], res[toks:2 * toks, LANES:2 * LANES]
            tile = jnp.where(low, top_a, bot_b) + pltpu.roll(jnp.where(low, top_b, bot_a), BLK, 1)
            psend[tt, :, v * LANES:(v + 1) * LANES] = tile.astype(BF16)
            dacc[...] += dot(gd[u], bw[v], NT)
        return carry

    def columns_and_send(i, carry):
        columns(i, carry)
        part_copy(tpeer(i)).start()
        return carry

    dacc[...] = jnp.zeros_like(dacc)

    def hidden_gradient():
        for lo in range(0, units, 256):
            size = min(256, units - lo)
            even = dacc[0:toks, lo // 2:(lo + size) // 2].astype(BF16)
            odd = dacc[toks:2 * toks, lo // 2:(lo + size) // 2].astype(BF16)
            dh_ref[:, lo:lo + size] = (
                dot(even, pick_units(0, (size // 2, size), 1))
                + dot(odd, pick_units(1, (size // 2, size), 1))
            ).astype(BF16)

    def weights_event(e):
        a, j = events[e]
        w_arrived_right(a, j).wait_recv()
        if a < h - 1 and j < chunks(a + 1):
            w_right(a + 1, j).start()
        w_arrived_left(a, other(j)).wait_recv()
        if a < h - 1 and j < chunks(a + 1):
            w_left(a + 1, other(j)).start()
        if j == chunks(a) - 1:
            w_sib(1 + a, c).start()
            w_sib(1 + h + a, c).start()

    def sums_event(e):
        s, j = hops[e]
        if e == 0:
            wait_sums(0)
        combine(s, j)
        if j == 0 and s + 2 <= h:
            pick(chip(h - s - 2))
            if s + 2 < h:
                pick(chip(s + 2 - h))
        if j == chunks(h - 1 if s == 0 else 0) - 1:
            wait_sums(s + 1)

    events = [(a, j) for a in range(h) for j in range(chunks(a))]
    hops = [(s, j) for s in range(h) for j in range(K // 2 if s == 0 else K)]
    n = len(events)
    first, last = (n + 1) // 4, 2 * n // 3
    for e in range(n):
        weights_event(e)
        if e == 0:
            split_hidden()
        if e == min(2, last - 1):
            positions()
        if first <= e < last:
            products((e - first) * n_t // (last - first), (e + 1 - first) * n_t // (last - first))
        if e == last - 1:
            pick(chip(h))
            pick(chip(h - 1))
            pick(chip(1 - h))
        if e >= last:
            sums_event(e - last)

    for k in range(2 * h + 1):
        w_sib(k, 1 - c).wait_recv()
    begin = n - last
    end = max(begin + 1, n - 2)
    for e in range(begin, n):
        sums_event(e)
        if begin <= e < end:
            lo, hi = (e - begin) * n_t // (end - begin), (e + 1 - begin) * n_t // (end - begin)
            if hi == n_t:
                if hi - 1 > lo:
                    lax.fori_loop(1 + lo, n_t, columns_and_send, 0)
                columns(0, 0)
            elif hi > lo:
                lax.fori_loop(1 + lo, 1 + hi, columns_and_send, 0)
        if e == n - 1:
            hidden_gradient()

    proj_acc = psend[t].astype(F32)
    for i in range(1, n_t):
        peer = tpeer(i)
        part_arrival(peer).wait_recv()
        proj_acc += parts[peer].astype(F32)
    proj_ref[...] = proj_acc.astype(BF16)

    for j in range(K):
        right_copy(h - 1, j).wait_recv()
        left_copy(h - 1, j).wait_recv()
    grads = g_own[z].astype(F32) + ring_r[h - 1].astype(F32) + ring_l[h - 1].astype(F32)
    flat[...] = grads.reshape(cap * HALF, LANES)
    scale = 1.0 / math.sqrt(toks * n_f)
    for i in range(HALF):
        piece = flat[pl.ds(i, cap, stride=HALF), :]
        gs_ref[0, :, i * LANES:(i + 1) * LANES] = jnp.where(live, piece * scale, 0.0)

    def sent_f(i, carry):
        ids_copy(i).wait_send()
        return carry

    def sent_t(i, carry):
        grad_copy(i).wait_send()
        part_copy(tpeer(i)).wait_send()
        return carry

    lax.fori_loop(1, n_f, sent_f, 0)
    lax.fori_loop(1, n_t, sent_t, 0)
    for s, j in events:
        w_right(s, j).wait_send()
        w_left(s, other(j)).wait_send()
    for s, j in hops:
        right_copy(s, j).wait_send()
        left_copy(s, other(j)).wait_send()
    for k in range(2 * h + 1):
        w_sib(k, c).wait_send()

    def sent_g(d, carry):
        g_copy(d).wait_send()
        return carry

    lax.fori_loop(0, n_z, sent_g, 0)


def finish(proj_ref, dh_ref, gs_ref, proj_out, dh_out, gs_out):
    proj_out[...] = proj_ref[...]
    dh_out[...] = dh_ref[...]
    gs_out[...] = gs_ref[...]


def on_device(hidden, grad_out, weight_slots, block_ids, slot_count):
    n_f, n_t = lax.axis_size("fsdp"), lax.axis_size("tensor")
    toks, units = hidden.shape
    cols = grad_out.shape[1]
    cap = weight_slots.shape[1]
    n_z = n_f // 2
    h = n_z // 2
    brows, bcols = units // BLK, n_t * cols // BLK
    block = (cap, HALF, LANES)
    dma = pltpu.SemaphoreType.DMA
    vmem = pl.BlockSpec(memory_space=pltpu.VMEM)
    groups = -(-brows * bcols // LANES)
    projected, d_hidden, grads = pl.pallas_call(
        functools.partial(kernel, n_f, n_t),
        out_shape=(
            jax.ShapeDtypeStruct((toks, cols), BF16),
            jax.ShapeDtypeStruct((toks, units), BF16),
            jax.ShapeDtypeStruct((1, cap, BLK * BLK), F32),
        ),
        in_specs=[vmem] * 4 + [pl.BlockSpec(memory_space=pltpu.SMEM)],
        out_specs=(vmem, vmem, vmem),
        scratch_shapes=[
            pltpu.VMEM((n_f * cap + 8, HALF, LANES), BF16),
            pltpu.VMEM((cap * HALF, LANES), F32),
            pltpu.VMEM(block, BF16),
            pltpu.VMEM((n_f, cap), jnp.int32),
            pltpu.VMEM((n_t, toks, cols), BF16),
            pltpu.VMEM((units // 2, 2 * toks), BF16),
            pltpu.VMEM((2 * toks, units // 2), BF16),
            pltpu.VMEM((2 * n_t, 2 * toks, 2 * LANES), BF16),
            pltpu.VMEM((brows * bcols, HALF, LANES), BF16),
            pltpu.VMEM((2, units // 2, 2 * LANES), BF16),
            pltpu.VMEM((n_z,) + block, BF16),
            pltpu.VMEM((n_z,) + block, BF16),
            pltpu.VMEM((n_z,) + block, BF16),
            pltpu.VMEM((h,) + block, BF16),
            pltpu.VMEM((h,) + block, BF16),
            pltpu.VMEM((h,) + block, BF16),
            pltpu.VMEM((h,) + block, BF16),
            pltpu.VMEM((n_t, toks, cols), BF16),
            pltpu.VMEM((n_t, toks, cols), BF16),
            pltpu.VMEM((2 * toks, units // 2), F32),
            pltpu.VMEM((groups, LANES), jnp.int32),
            pltpu.SMEM((groups, LANES), jnp.int32),
            pltpu.SMEM((n_f, cap), jnp.int32),
            dma((n_f,)), dma((n_f,)), dma((n_t,)), dma((n_t,)),
            dma((h, K)), dma((h, K)), dma((h, K)), dma((h, K)),
            dma((2 * h + 1,)), dma((2 * h + 1,)),
            dma((n_z,)), dma((n_z,)),
            dma((h, K)), dma((h, K)), dma((h, K)), dma((h, K)),
            dma((n_t,)), dma((n_t,)), dma((2,)),
        ],
        compiler_params=pltpu.CompilerParams(
            collective_id=0, has_side_effects=True, vmem_limit_bytes=56 * 1024 * 1024
        ),
        cost_estimate=pl.CostEstimate(
            flops=10 * toks * units * n_t * cols, bytes_accessed=2 * 1024 * 1024, transcendentals=0
        ),
    )(hidden, grad_out, weight_slots, block_ids, slot_count)
    return pl.pallas_call(
        finish,
        out_shape=tuple(jax.ShapeDtypeStruct(x.shape, x.dtype) for x in (projected, d_hidden, grads)),
        in_specs=[vmem] * 3,
        out_specs=(vmem, vmem, vmem),
    )(projected, d_hidden, grads)


def solution(mesh):
    in_specs = (
        P("fsdp", "tensor"),
        P("fsdp", "tensor"),
        P("tensor", "fsdp", None),
        P("tensor", "fsdp"),
        P("tensor", "fsdp"),
    )
    out_specs = (P("fsdp", "tensor"), P("fsdp", "tensor"), P("tensor", "fsdp", None))
    return jax.shard_map(
        on_device, mesh=mesh, in_specs=in_specs, out_specs=out_specs, check_vma=False
    )
```

```python
import functools
import math

import jax
import jax.numpy as jnp
from jax import lax
from jax.experimental import pallas as pl
from jax.experimental.pallas import tpu as pltpu
from jax.sharding import PartitionSpec as P

BLK = 64
HALF = BLK // 2
LANES = 2 * BLK
MESH = pl.DeviceIdType.MESH
F32 = jnp.float32
BF16 = jnp.bfloat16
K = 2
NN = (((1,), (0,)), ((), ()))
NT = (((1,), (1,)), ((), ()))


def dot(a, b, dims=NN):
    return lax.dot_general(a, b, dims, preferred_element_type=F32)


def lane_iota(shape):
    return lax.broadcasted_iota(jnp.int32, shape, 1)


def kernel(
    n_f, n_t,
    hid_ref, grad_ref, slots_ref, ids_ref, count_ref,
    proj_ref, dh_ref, gs_ref,
    wall, flat, w_ref, ids_all, fg, h2, hm, gd, q, bw,
    g_own, g_oth, g_sib, ring_r, ring_l, send_r, send_l,
    parts, psend, dacc, inv_v, inv_s, ids_s,
    ids_ss, ids_rs, gr_ss, gr_rs, wr_ss, wr_rs, wl_ss, wl_rs, wb_ss, wb_rs,
    gs_ss, gs_rs, rr_ss, rr_rs, rl_ss, rl_rs, pp_ss, pp_rs, loc_s,
):
    cap = slots_ref.shape[1]
    half, step = cap // 2, cap // K
    toks, units = hid_ref.shape
    cols = grad_ref.shape[1]
    brows = units // BLK
    rows = units // 2
    bcols = n_t * cols // BLK
    n_z = n_f // 2
    h = n_z // 2
    empty = n_f * cap

    f = lax.axis_index("fsdp")
    t = lax.axis_index("tensor")
    z, c = f // 2, f % 2

    def chip(offset):
        return lax.rem(z + offset + n_z, n_z)

    right, left, sib = chip(1) * 2 + c, chip(-1) * 2 + c, z * 2 + 1 - c

    def fpeer(i):
        return lax.rem(f + i, n_f)

    def tpeer(i):
        return lax.rem(t + i, n_t)

    def to_f(src, dst, ss, rs, peer):
        return pltpu.make_async_remote_copy(
            src_ref=src, dst_ref=dst, send_sem=ss, recv_sem=rs,
            device_id={"fsdp": peer}, device_id_type=MESH,
        )

    def to_t(src, dst, ss, rs, peer):
        return pltpu.make_async_remote_copy(
            src_ref=src, dst_ref=dst, send_sem=ss, recv_sem=rs,
            device_id={"tensor": peer}, device_id_type=MESH,
        )

    barrier = pltpu.get_barrier_semaphore()

    def greet_f(i, carry):
        pl.semaphore_signal(barrier, inc=1, device_id={"fsdp": fpeer(i)}, device_id_type=MESH)
        return carry

    def greet_t(i, carry):
        pl.semaphore_signal(barrier, inc=1, device_id={"tensor": tpeer(i)}, device_id_type=MESH)
        return carry

    lax.fori_loop(1, n_f, greet_f, 0)
    lax.fori_loop(1, n_t, greet_t, 0)
    live = lax.broadcasted_iota(jnp.int32, (cap, LANES), 0) < count_ref[0, 0]
    for i in range(HALF):
        piece = slots_ref[0, :, i * LANES:(i + 1) * LANES].astype(F32)
        flat[pl.ds(i, cap, stride=HALF), :] = jnp.where(live, piece, 0.0)
    w_ref[...] = flat[...].reshape(cap, HALF, LANES).astype(BF16)

    def w_part(zz, cc, lo, size):
        return wall.at[pl.ds((zz * 2 + cc) * cap + lo, size)]

    def w_right(s, j):
        dst = w_part(chip(-s), c, j * step, step)
        src = w_ref.at[pl.ds(j * step, step)] if s == 0 else dst
        return to_f(src, dst, wr_ss.at[s, j], wr_rs.at[s, j], right)

    def w_left(s, j):
        dst = w_part(chip(s), c, j * step, step)
        src = w_ref.at[pl.ds(j * step, step)] if s == 0 else dst
        return to_f(src, dst, wl_ss.at[s, j], wl_rs.at[s, j], left)

    def w_arrived_right(a, j):
        ref = w_part(chip(-1 - a), c, j * step, step)
        return to_f(ref, ref, wr_ss.at[a, j], wr_rs.at[a, j], right)

    def w_arrived_left(a, j):
        ref = w_part(chip(1 + a), c, j * step, step)
        return to_f(ref, ref, wl_ss.at[a, j], wl_rs.at[a, j], left)

    def w_sib(k, core):
        if k == 0:
            dst = w_part(z, core, 0, cap)
            src = w_ref if core is c else dst
        elif k <= h:
            a = k - 1
            src = dst = w_part(chip(-1 - a), core, 0, half if a == h - 1 else cap)
        else:
            a = k - 1 - h
            lo, size = (half, half) if a == h - 1 else (0, cap)
            src = dst = w_part(chip(1 + a), core, lo, size)
        return to_f(src, dst, wb_ss.at[k], wb_rs.at[k], sib)

    def ids_copy(i):
        return to_f(ids_ref, ids_all.at[pl.ds(f, 1)], ids_ss.at[i], ids_rs.at[f], fpeer(i))

    def ids_arrival(i):
        peer = fpeer(i)
        ref = ids_all.at[pl.ds(peer, 1)]
        return to_f(ref, ref, ids_ss.at[i], ids_rs.at[peer], peer)

    def grad_copy(i):
        return to_t(grad_ref, fg.at[t], gr_ss.at[i], gr_rs.at[t], tpeer(i))

    def grad_arrival(peer):
        return to_t(fg.at[peer], fg.at[peer], gr_ss.at[0], gr_rs.at[peer], peer)

    def chunks(s):
        return K // 2 if s == h - 1 else K

    def other(j):
        return (j + K // 2) % K

    def start_ids(i, carry):
        ids_copy(i).start()
        return carry

    def start_grad(i, carry):
        grad_copy(i).start()
        return carry

    pl.semaphore_wait(barrier, n_f + n_t - 2)
    for j in range(chunks(0)):
        w_right(0, j).start()
        w_left(0, other(j)).start()
    w_sib(0, c).start()

    lax.fori_loop(1, n_t, start_grad, 0)
    lax.fori_loop(1, n_f, start_ids, 0)

    wall[pl.ds(f * cap, cap)] = w_ref[...]
    wall[pl.ds(empty, 8)] = jnp.zeros((8, HALF, LANES), BF16)
    ids_all[pl.ds(f, 1), :] = ids_ref[...]
    fg[t] = grad_ref[...]

    def pick_units(odd, shape, unit_axis):
        unit = lax.broadcasted_iota(jnp.int32, shape, unit_axis)
        out = lax.broadcasted_iota(jnp.int32, shape, 1 - unit_axis)
        return jnp.where(unit == 2 * out + odd, 1.0, 0.0).astype(BF16)

    def split_hidden():
        for lo in range(0, units, 256):
            size = min(256, units - lo)
            chunk = hid_ref[:, lo:lo + size]
            for odd in range(2):
                sel = pick_units(odd, (size // 2, size), 1)
                h2[lo // 2:(lo + size) // 2, odd * toks:(odd + 1) * toks] = dot(sel, chunk, NT).astype(BF16)
                hm[odd * toks:(odd + 1) * toks, lo // 2:(lo + size) // 2] = dot(chunk, sel, NT).astype(BF16)

    def positions():
        def wait_ids(i, carry):
            ids_arrival(i).wait_recv()
            return carry

        lax.fori_loop(1, n_f, wait_ids, 0)
        lane = lane_iota((cap, LANES))
        diagonal = lane_iota((cap, cap)) == lax.broadcasted_iota(jnp.int32, (cap, cap), 0)
        row = lax.broadcasted_iota(jnp.int32, (cap, LANES), 0)
        groups = -(-brows * bcols // LANES)

        def owner(j, accs):
            x = jnp.sum(jnp.where(diagonal, ids_all[pl.ds(j, 1), :], 0), axis=1, keepdims=True)
            slot = row + j * cap
            return tuple(
                jnp.minimum(acc, jnp.where(x == lane + p * LANES, slot, empty))
                for p, acc in enumerate(accs)
            )

        accs = lax.fori_loop(
            0, n_f, owner, tuple(jnp.full((cap, LANES), empty, jnp.int32) for _ in range(groups))
        )
        for p, acc in enumerate(accs):
            inv_v[p:p + 1, :] = jnp.min(acc, axis=0, keepdims=True)
        one = pltpu.make_async_copy(inv_v, inv_s, loc_s.at[0])
        two = pltpu.make_async_copy(ids_all, ids_s, loc_s.at[1])
        one.start()
        two.start()
        one.wait()
        two.wait()

    def product(i, carry):
        tt = lax.rem(t - i + n_t, n_t)
        low = lane_iota((toks, LANES)) < BLK
        for v in range(2):
            u = 2 * tt + v
            src = fg[tt, :, v * LANES:(v + 1) * LANES].astype(F32)
            swapped = pltpu.roll(src, BLK, 1)
            gd[u, 0:toks, 0:LANES] = jnp.where(low, src, 0.0).astype(BF16)
            gd[u, toks:2 * toks, 0:LANES] = jnp.where(low, 0.0, swapped).astype(BF16)
            gd[u, 0:toks, LANES:2 * LANES] = jnp.where(low, swapped, 0.0).astype(BF16)
            gd[u, toks:2 * toks, LANES:2 * LANES] = jnp.where(low, 0.0, src).astype(BF16)
            res = dot(h2[...], gd[u]).astype(BF16)
            for r in range(brows):
                q[r * bcols + 2 * u] = res[r * HALF:(r + 1) * HALF, 0:LANES]
                q[r * bcols + 2 * u + 1] = res[r * HALF:(r + 1) * HALF, LANES:2 * LANES]
        return carry

    def products(lo, hi):
        if lo == 0 and hi > 0:
            product(0, 0)
            lo = 1

        def arrived(i, carry):
            grad_arrival(lax.rem(t - i + n_t, n_t)).wait_recv()
            return product(i, carry)

        if hi > lo:
            lax.fori_loop(lo, hi, arrived, 0)

    def pick(d):
        def one(i, carry):
            g_own[d, i] = q[ids_s[2 * d + c, i]]
            g_oth[d, i] = q[ids_s[2 * d + 1 - c, i]]
            return carry

        lax.fori_loop(0, cap, one, 0, unroll=8)
        g_copy(d).start()

    def g_copy(d):
        return to_f(g_oth.at[d], g_sib.at[d], gs_ss.at[d], gs_rs.at[d], sib)

    def right_copy(s, j):
        part = pl.ds(j * step, step)
        return to_f(send_r.at[s, part], ring_r.at[s, part], rr_ss.at[s, j], rr_rs.at[s, j], right)

    def left_copy(s, j):
        part = pl.ds(j * step, step)
        return to_f(send_l.at[s, part], ring_l.at[s, part], rl_ss.at[s, j], rl_rs.at[s, j], left)

    def wait_sums(s):
        for d in [chip(h - s)] if s in (0, h) else [chip(h - s), chip(s - h)]:
            g_copy(d).wait_recv()
            g_own[d] = g_own[d] + g_sib[d]

    def combine(s, j):
        arrives = s > 1 or (s == 1 and j < K // 2)
        part = pl.ds(j * step, step)
        if arrives:
            right_copy(s - 1, j).wait_recv()
        value = g_own[chip(h - s), part]
        send_r[s, part] = value + ring_r[s - 1, part] if arrives else value
        right_copy(s, j).start()
        j = other(j)
        part = pl.ds(j * step, step)
        if arrives:
            left_copy(s - 1, j).wait_recv()
        value = g_own[chip(s - h), part]
        send_l[s, part] = value + ring_l[s - 1, part] if arrives else value
        left_copy(s, j).start()

    def part_copy(peer):
        return to_t(psend.at[peer], parts.at[t], pp_ss.at[peer], pp_rs.at[t], peer)

    def part_arrival(peer):
        return to_t(parts.at[peer], parts.at[peer], pp_ss.at[peer], pp_rs.at[peer], peer)

    def columns(i, carry):
        tt = tpeer(i)
        low = lane_iota((toks, LANES)) < BLK
        for v in range(2):
            u = tt * 2 + v
            for r in range(brows):
                for side in range(2):
                    pos = r * bcols + 2 * u + side
                    bw[v, r * HALF:(r + 1) * HALF, side * LANES:(side + 1) * LANES] = wall[
                        inv_s[lax.div(pos, LANES), lax.rem(pos, LANES)]
                    ]
            res = dot(hm[...], bw[v])
            top_a, top_b = res[0:toks, 0:LANES], res[0:toks, LANES:2 * LANES]
            bot_a, bot_b = res[toks:2 * toks, 0:LANES], res[toks:2 * toks, LANES:2 * LANES]
            tile = jnp.where(low, top_a, bot_b) + pltpu.roll(jnp.where(low, top_b, bot_a), BLK, 1)
            psend[tt, :, v * LANES:(v + 1) * LANES] = tile.astype(BF16)
            dacc[...] += dot(gd[u], bw[v], NT)
        return carry

    def columns_and_send(i, carry):
        columns(i, carry)
        part_copy(tpeer(i)).start()
        return carry

    dacc[...] = jnp.zeros_like(dacc)

    def hidden_gradient():
        for lo in range(0, units, 256):
            size = min(256, units - lo)
            even = dacc[0:toks, lo // 2:(lo + size) // 2].astype(BF16)
            odd = dacc[toks:2 * toks, lo // 2:(lo + size) // 2].astype(BF16)
            dh_ref[:, lo:lo + size] = (
                dot(even, pick_units(0, (size // 2, size), 1))
                + dot(odd, pick_units(1, (size // 2, size), 1))
            ).astype(BF16)

    def weights_event(e):
        a, j = events[e]
        w_arrived_right(a, j).wait_recv()
        if a < h - 1 and j < chunks(a + 1):
            w_right(a + 1, j).start()
        w_arrived_left(a, other(j)).wait_recv()
        if a < h - 1 and j < chunks(a + 1):
            w_left(a + 1, other(j)).start()
        if j == chunks(a) - 1:
            w_sib(1 + a, c).start()
            w_sib(1 + h + a, c).start()

    def sums_event(e):
        s, j = hops[e]
        if e == 0:
            wait_sums(0)
        combine(s, j)
        if j == 0 and s + 2 <= h:
            pick(chip(h - s - 2))
            if s + 2 < h:
                pick(chip(s + 2 - h))
        if j == chunks(h - 1 if s == 0 else 0) - 1:
            wait_sums(s + 1)

    events = [(a, j) for a in range(h) for j in range(chunks(a))]
    hops = [(s, j) for s in range(h) for j in range(K // 2 if s == 0 else K)]
    n = len(events)
    first, last = (n + 1) // 4, 2 * n // 3
    for e in range(n):
        weights_event(e)
        if e == 0:
            split_hidden()
        if e == min(2, last - 1):
            positions()
        if first <= e < last:
            products((e - first) * n_t // (last - first), (e + 1 - first) * n_t // (last - first))
        if e == last - 1:
            pick(chip(h))
            pick(chip(h - 1))
            pick(chip(1 - h))
        if e >= last:
            sums_event(e - last)

    for k in range(2 * h + 1):
        w_sib(k, 1 - c).wait_recv()
    begin = n - last
    end = max(begin + 1, n - 2)
    for e in range(begin, n):
        sums_event(e)
        if begin <= e < end:
            lo, hi = (e - begin) * n_t // (end - begin), (e + 1 - begin) * n_t // (end - begin)
            if hi == n_t:
                if hi - 1 > lo:
                    lax.fori_loop(1 + lo, n_t, columns_and_send, 0)
                columns(0, 0)
            elif hi > lo:
                lax.fori_loop(1 + lo, 1 + hi, columns_and_send, 0)
        if e == n - 1:
            hidden_gradient()

    proj_acc = psend[t].astype(F32)
    for i in range(1, n_t):
        peer = tpeer(i)
        part_arrival(peer).wait_recv()
        proj_acc += parts[peer].astype(F32)
    proj_ref[...] = proj_acc.astype(BF16)

    def sent_f(i, carry):
        ids_copy(i).wait_send()
        return carry

    def sent_t(i, carry):
        grad_copy(i).wait_send()
        part_copy(tpeer(i)).wait_send()
        return carry

    def sent_g(d, carry):
        g_copy(d).wait_send()
        return carry

    lax.fori_loop(1, n_f, sent_f, 0)
    lax.fori_loop(1, n_t, sent_t, 0)
    lax.fori_loop(0, n_z, sent_g, 0)
    for k in range(2 * h + 1):
        w_sib(k, c).wait_send()
    for s, j in events:
        w_right(s, j).wait_send()
        w_left(s, other(j)).wait_send()
    for s, j in hops:
        right_copy(s, j).wait_send()
        left_copy(s, other(j)).wait_send()

    for j in range(K):
        right_copy(h - 1, j).wait_recv()
        left_copy(h - 1, j).wait_recv()
    grads = g_own[z].astype(F32) + ring_r[h - 1].astype(F32) + ring_l[h - 1].astype(F32)
    flat[...] = grads.reshape(cap * HALF, LANES)
    scale = 1.0 / math.sqrt(toks * n_f)
    for i in range(HALF):
        piece = flat[pl.ds(i, cap, stride=HALF), :]
        gs_ref[0, :, i * LANES:(i + 1) * LANES] = jnp.where(live, piece * scale, 0.0)


def on_device(hidden, grad_out, weight_slots, block_ids, slot_count):
    n_f, n_t = lax.axis_size("fsdp"), lax.axis_size("tensor")
    toks, units = hidden.shape
    cols = grad_out.shape[1]
    cap = weight_slots.shape[1]
    n_z = n_f // 2
    h = n_z // 2
    brows, bcols = units // BLK, n_t * cols // BLK
    block = (cap, HALF, LANES)
    dma = pltpu.SemaphoreType.DMA
    vmem = pl.BlockSpec(memory_space=pltpu.VMEM)
    groups = -(-brows * bcols // LANES)
    projected, d_hidden, grads = pl.pallas_call(
        functools.partial(kernel, n_f, n_t),
        out_shape=(
            pltpu.VMEM((toks, cols), BF16),
            pltpu.VMEM((toks, units), BF16),
            pltpu.VMEM((1, cap, BLK * BLK), F32),
        ),
        in_specs=[vmem] * 4 + [pl.BlockSpec(memory_space=pltpu.SMEM)],
        out_specs=(vmem, vmem, vmem),
        scratch_shapes=[
            pltpu.VMEM((n_f * cap + 8, HALF, LANES), BF16),
            pltpu.VMEM((cap * HALF, LANES), F32),
            pltpu.VMEM(block, BF16),
            pltpu.VMEM((n_f, cap), jnp.int32),
            pltpu.VMEM((n_t, toks, cols), BF16),
            pltpu.VMEM((units // 2, 2 * toks), BF16),
            pltpu.VMEM((2 * toks, units // 2), BF16),
            pltpu.VMEM((2 * n_t, 2 * toks, 2 * LANES), BF16),
            pltpu.VMEM((brows * bcols, HALF, LANES), BF16),
            pltpu.VMEM((2, units // 2, 2 * LANES), BF16),
            pltpu.VMEM((n_z,) + block, BF16),
            pltpu.VMEM((n_z,) + block, BF16),
            pltpu.VMEM((n_z,) + block, BF16),
            pltpu.VMEM((h,) + block, BF16),
            pltpu.VMEM((h,) + block, BF16),
            pltpu.VMEM((h,) + block, BF16),
            pltpu.VMEM((h,) + block, BF16),
            pltpu.VMEM((n_t, toks, cols), BF16),
            pltpu.VMEM((n_t, toks, cols), BF16),
            pltpu.VMEM((2 * toks, units // 2), F32),
            pltpu.VMEM((groups, LANES), jnp.int32),
            pltpu.SMEM((groups, LANES), jnp.int32),
            pltpu.SMEM((n_f, cap), jnp.int32),
            dma((n_f,)), dma((n_f,)), dma((n_t,)), dma((n_t,)),
            dma((h, K)), dma((h, K)), dma((h, K)), dma((h, K)),
            dma((2 * h + 1,)), dma((2 * h + 1,)),
            dma((n_z,)), dma((n_z,)),
            dma((h, K)), dma((h, K)), dma((h, K)), dma((h, K)),
            dma((n_t,)), dma((n_t,)), dma((2,)),
        ],
        compiler_params=pltpu.CompilerParams(
            collective_id=0, has_side_effects=True, vmem_limit_bytes=56 * 1024 * 1024
        ),
        cost_estimate=pl.CostEstimate(
            flops=10 * toks * units * n_t * cols, bytes_accessed=2 * 1024 * 1024, transcendentals=0
        ),
    )(hidden, grad_out, weight_slots, block_ids, slot_count)
    return (projected, d_hidden, grads)


def solution(mesh):
    in_specs = (
        P("fsdp", "tensor"),
        P("fsdp", "tensor"),
        P("tensor", "fsdp", None),
        P("tensor", "fsdp"),
        P("tensor", "fsdp"),
    )
    out_specs = (P("fsdp", "tensor"), P("fsdp", "tensor"), P("tensor", "fsdp", None))
    return jax.shard_map(
        on_device, mesh=mesh, in_specs=in_specs, out_specs=out_specs, check_vma=False
    )
```

```python
import functools
import math

import jax
import jax.numpy as jnp
from jax import lax
from jax.experimental import pallas as pl
from jax.experimental.pallas import tpu as pltpu
from jax.sharding import PartitionSpec as P

BLK = 64
HALF = BLK // 2
LANES = 2 * BLK
MESH = pl.DeviceIdType.MESH
F32 = jnp.float32
BF16 = jnp.bfloat16
K = 2
NN = (((1,), (0,)), ((), ()))
NT = (((1,), (1,)), ((), ()))


def dot(a, b, dims=NN):
    return lax.dot_general(a, b, dims, preferred_element_type=F32)


def lane_iota(shape):
    return lax.broadcasted_iota(jnp.int32, shape, 1)


def kernel(
    n_f, n_t,
    hid_ref, grad_ref, slots_ref, ids_ref, count_ref,
    proj_ref, dh_ref, gs_ref,
    wall, flat, w_ref, ids_all, fg, h2, hm, gd, q, bw,
    g_own, g_oth, g_sib, ring_r, ring_l, send_r, send_l,
    parts, psend, dacc, inv_v, inv_s, ids_s,
    ids_ss, ids_rs, gr_ss, gr_rs, wr_ss, wr_rs, wl_ss, wl_rs, wb_ss, wb_rs,
    gs_ss, gs_rs, rr_ss, rr_rs, rl_ss, rl_rs, pp_ss, pp_rs, loc_s,
):
    cap = slots_ref.shape[1]
    half, step = cap // 2, cap // K
    toks, units = hid_ref.shape
    cols = grad_ref.shape[1]
    brows = units // BLK
    rows = units // 2
    bcols = n_t * cols // BLK
    n_z = n_f // 2
    h = n_z // 2
    empty = n_f * cap

    f = lax.axis_index("fsdp")
    t = lax.axis_index("tensor")
    z, c = f // 2, f % 2

    def chip(offset):
        return lax.rem(z + offset + n_z, n_z)

    right, left, sib = chip(1) * 2 + c, chip(-1) * 2 + c, z * 2 + 1 - c

    def fpeer(i):
        return lax.rem(f + i, n_f)

    def tpeer(i):
        return lax.rem(t + i, n_t)

    def to_f(src, dst, ss, rs, peer):
        return pltpu.make_async_remote_copy(
            src_ref=src, dst_ref=dst, send_sem=ss, recv_sem=rs,
            device_id={"fsdp": peer}, device_id_type=MESH,
        )

    def to_t(src, dst, ss, rs, peer):
        return pltpu.make_async_remote_copy(
            src_ref=src, dst_ref=dst, send_sem=ss, recv_sem=rs,
            device_id={"tensor": peer}, device_id_type=MESH,
        )

    barrier = pltpu.get_barrier_semaphore()

    def greet_f(i, carry):
        pl.semaphore_signal(barrier, inc=1, device_id={"fsdp": fpeer(i)}, device_id_type=MESH)
        return carry

    def greet_t(i, carry):
        pl.semaphore_signal(barrier, inc=1, device_id={"tensor": tpeer(i)}, device_id_type=MESH)
        return carry

    lax.fori_loop(1, n_f, greet_f, 0)
    lax.fori_loop(1, n_t, greet_t, 0)
    live = lax.broadcasted_iota(jnp.int32, (cap, LANES), 0) < count_ref[0, 0]
    for i in range(HALF):
        piece = slots_ref[0, :, i * LANES:(i + 1) * LANES].astype(F32)
        flat[pl.ds(i, cap, stride=HALF), :] = jnp.where(live, piece, 0.0)
    w_ref[...] = flat[...].reshape(cap, HALF, LANES).astype(BF16)

    def w_part(zz, cc, lo, size):
        return wall.at[pl.ds((zz * 2 + cc) * cap + lo, size)]

    def w_right(s, j):
        dst = w_part(chip(-s), c, j * step, step)
        src = w_ref.at[pl.ds(j * step, step)] if s == 0 else dst
        return to_f(src, dst, wr_ss.at[s, j], wr_rs.at[s, j], right)

    def w_left(s, j):
        dst = w_part(chip(s), c, j * step, step)
        src = w_ref.at[pl.ds(j * step, step)] if s == 0 else dst
        return to_f(src, dst, wl_ss.at[s, j], wl_rs.at[s, j], left)

    def w_arrived_right(a, j):
        ref = w_part(chip(-1 - a), c, j * step, step)
        return to_f(ref, ref, wr_ss.at[a, j], wr_rs.at[a, j], right)

    def w_arrived_left(a, j):
        ref = w_part(chip(1 + a), c, j * step, step)
        return to_f(ref, ref, wl_ss.at[a, j], wl_rs.at[a, j], left)

    def w_sib(k, core):
        if k == 0:
            dst = w_part(z, core, 0, cap)
            src = w_ref if core is c else dst
        elif k <= h:
            a = k - 1
            src = dst = w_part(chip(-1 - a), core, 0, half if a == h - 1 else cap)
        else:
            a = k - 1 - h
            lo, size = (half, half) if a == h - 1 else (0, cap)
            src = dst = w_part(chip(1 + a), core, lo, size)
        return to_f(src, dst, wb_ss.at[k], wb_rs.at[k], sib)

    def ids_copy(i):
        return to_f(ids_ref, ids_all.at[pl.ds(f, 1)], ids_ss.at[i], ids_rs.at[f], fpeer(i))

    def ids_arrival(i):
        peer = fpeer(i)
        ref = ids_all.at[pl.ds(peer, 1)]
        return to_f(ref, ref, ids_ss.at[i], ids_rs.at[peer], peer)

    def grad_copy(i):
        return to_t(grad_ref, fg.at[t], gr_ss.at[i], gr_rs.at[t], tpeer(i))

    def grad_arrival(peer):
        return to_t(fg.at[peer], fg.at[peer], gr_ss.at[0], gr_rs.at[peer], peer)

    def chunks(s):
        return K // 2 if s == h - 1 else K

    def other(j):
        return (j + K // 2) % K

    def start_ids(i, carry):
        ids_copy(i).start()
        return carry

    def start_grad(i, carry):
        grad_copy(i).start()
        return carry

    pl.semaphore_wait(barrier, n_f + n_t - 2)
    for j in range(chunks(0)):
        w_right(0, j).start()
        w_left(0, other(j)).start()
    w_sib(0, c).start()

    lax.fori_loop(1, n_t, start_grad, 0)
    lax.fori_loop(1, n_f, start_ids, 0)

    wall[pl.ds(f * cap, cap)] = w_ref[...]
    wall[pl.ds(empty, 8)] = jnp.zeros((8, HALF, LANES), BF16)
    ids_all[pl.ds(f, 1), :] = ids_ref[...]
    fg[t] = grad_ref[...]

    def pick_units(odd, shape, unit_axis):
        unit = lax.broadcasted_iota(jnp.int32, shape, unit_axis)
        out = lax.broadcasted_iota(jnp.int32, shape, 1 - unit_axis)
        return jnp.where(unit == 2 * out + odd, 1.0, 0.0).astype(BF16)

    def split_hidden():
        for lo in range(0, units, 256):
            size = min(256, units - lo)
            chunk = hid_ref[:, lo:lo + size]
            for odd in range(2):
                sel = pick_units(odd, (size // 2, size), 1)
                h2[lo // 2:(lo + size) // 2, odd * toks:(odd + 1) * toks] = dot(sel, chunk, NT).astype(BF16)
                hm[odd * toks:(odd + 1) * toks, lo // 2:(lo + size) // 2] = dot(chunk, sel, NT).astype(BF16)

    def positions():
        def wait_ids(i, carry):
            ids_arrival(i).wait_recv()
            return carry

        lax.fori_loop(1, n_f, wait_ids, 0)
        lane = lane_iota((cap, LANES))
        diagonal = lane_iota((cap, cap)) == lax.broadcasted_iota(jnp.int32, (cap, cap), 0)
        row = lax.broadcasted_iota(jnp.int32, (cap, LANES), 0)
        groups = -(-brows * bcols // LANES)

        def owner(j, accs):
            x = jnp.sum(jnp.where(diagonal, ids_all[pl.ds(j, 1), :], 0), axis=1, keepdims=True)
            slot = row + j * cap
            return tuple(
                jnp.minimum(acc, jnp.where(x == lane + p * LANES, slot, empty))
                for p, acc in enumerate(accs)
            )

        accs = lax.fori_loop(
            0, n_f, owner, tuple(jnp.full((cap, LANES), empty, jnp.int32) for _ in range(groups))
        )
        for p, acc in enumerate(accs):
            inv_v[p:p + 1, :] = jnp.min(acc, axis=0, keepdims=True)
        one = pltpu.make_async_copy(inv_v, inv_s, loc_s.at[0])
        two = pltpu.make_async_copy(ids_all, ids_s, loc_s.at[1])
        one.start()
        two.start()
        one.wait()
        two.wait()

    def product(i, carry):
        tt = lax.rem(t - i + n_t, n_t)
        low = lane_iota((toks, LANES)) < BLK
        for v in range(2):
            u = 2 * tt + v
            src = fg[tt, :, v * LANES:(v + 1) * LANES].astype(F32)
            swapped = pltpu.roll(src, BLK, 1)
            gd[u, 0:toks, 0:LANES] = jnp.where(low, src, 0.0).astype(BF16)
            gd[u, toks:2 * toks, 0:LANES] = jnp.where(low, 0.0, swapped).astype(BF16)
            gd[u, 0:toks, LANES:2 * LANES] = jnp.where(low, swapped, 0.0).astype(BF16)
            gd[u, toks:2 * toks, LANES:2 * LANES] = jnp.where(low, 0.0, src).astype(BF16)
            res = dot(h2[...], gd[u]).astype(BF16)
            for r in range(brows):
                q[r * bcols + 2 * u] = res[r * HALF:(r + 1) * HALF, 0:LANES]
                q[r * bcols + 2 * u + 1] = res[r * HALF:(r + 1) * HALF, LANES:2 * LANES]
        return carry

    def products(lo, hi):
        if lo == 0 and hi > 0:
            product(0, 0)
            lo = 1

        def arrived(i, carry):
            grad_arrival(lax.rem(t - i + n_t, n_t)).wait_recv()
            return product(i, carry)

        if hi > lo:
            lax.fori_loop(lo, hi, arrived, 0)

    def pick(d):
        for core, buf in ((c, g_own), (1 - c, g_oth)):
            for lo in range(0, cap, 8):
                blocks = [q[ids_s[2 * d + core, i]] for i in range(lo, lo + 8)]
                for i, value in enumerate(blocks):
                    buf[d, lo + i] = value
        g_copy(d).start()

    def g_copy(d):
        return to_f(g_oth.at[d], g_sib.at[d], gs_ss.at[d], gs_rs.at[d], sib)

    def right_copy(s, j):
        part = pl.ds(j * step, step)
        return to_f(send_r.at[s, part], ring_r.at[s, part], rr_ss.at[s, j], rr_rs.at[s, j], right)

    def left_copy(s, j):
        part = pl.ds(j * step, step)
        return to_f(send_l.at[s, part], ring_l.at[s, part], rl_ss.at[s, j], rl_rs.at[s, j], left)

    def wait_sums(s):
        for d in [chip(h - s)] if s in (0, h) else [chip(h - s), chip(s - h)]:
            g_copy(d).wait_recv()
            g_own[d] = g_own[d] + g_sib[d]

    def combine(s, j):
        arrives = s > 1 or (s == 1 and j < K // 2)
        part = pl.ds(j * step, step)
        if arrives:
            right_copy(s - 1, j).wait_recv()
        value = g_own[chip(h - s), part]
        send_r[s, part] = value + ring_r[s - 1, part] if arrives else value
        right_copy(s, j).start()
        j = other(j)
        part = pl.ds(j * step, step)
        if arrives:
            left_copy(s - 1, j).wait_recv()
        value = g_own[chip(s - h), part]
        send_l[s, part] = value + ring_l[s - 1, part] if arrives else value
        left_copy(s, j).start()

    def part_copy(peer):
        return to_t(psend.at[peer], parts.at[t], pp_ss.at[peer], pp_rs.at[t], peer)

    def part_arrival(peer):
        return to_t(parts.at[peer], parts.at[peer], pp_ss.at[peer], pp_rs.at[peer], peer)

    def columns(i, carry):
        tt = tpeer(i)
        low = lane_iota((toks, LANES)) < BLK
        for v in range(2):
            u = tt * 2 + v
            for r in range(brows):
                for side in range(2):
                    pos = r * bcols + 2 * u + side
                    bw[v, r * HALF:(r + 1) * HALF, side * LANES:(side + 1) * LANES] = wall[
                        inv_s[lax.div(pos, LANES), lax.rem(pos, LANES)]
                    ]
            res = dot(hm[...], bw[v])
            top_a, top_b = res[0:toks, 0:LANES], res[0:toks, LANES:2 * LANES]
            bot_a, bot_b = res[toks:2 * toks, 0:LANES], res[toks:2 * toks, LANES:2 * LANES]
            tile = jnp.where(low, top_a, bot_b) + pltpu.roll(jnp.where(low, top_b, bot_a), BLK, 1)
            psend[tt, :, v * LANES:(v + 1) * LANES] = tile.astype(BF16)
            dacc[...] += dot(gd[u], bw[v], NT)
        return carry

    def columns_and_send(i, carry):
        columns(i, carry)
        part_copy(tpeer(i)).start()
        return carry

    dacc[...] = jnp.zeros_like(dacc)

    def hidden_gradient():
        for lo in range(0, units, 256):
            size = min(256, units - lo)
            even = dacc[0:toks, lo // 2:(lo + size) // 2].astype(BF16)
            odd = dacc[toks:2 * toks, lo // 2:(lo + size) // 2].astype(BF16)
            dh_ref[:, lo:lo + size] = (
                dot(even, pick_units(0, (size // 2, size), 1))
                + dot(odd, pick_units(1, (size // 2, size), 1))
            ).astype(BF16)

    def weights_event(e):
        a, j = events[e]
        w_arrived_right(a, j).wait_recv()
        if a < h - 1 and j < chunks(a + 1):
            w_right(a + 1, j).start()
        w_arrived_left(a, other(j)).wait_recv()
        if a < h - 1 and j < chunks(a + 1):
            w_left(a + 1, other(j)).start()
        if j == chunks(a) - 1:
            w_sib(1 + a, c).start()
            w_sib(1 + h + a, c).start()

    def sums_event(e):
        s, j = hops[e]
        if e == 0:
            wait_sums(0)
        combine(s, j)
        if j == chunks(h - 1 if s == 0 else 0) - 1:
            wait_sums(s + 1)
            if s + 2 <= h:
                pick(chip(h - s - 2))
                if s + 2 < h:
                    pick(chip(s + 2 - h))

    events = [(a, j) for a in range(h) for j in range(chunks(a))]
    hops = [(s, j) for s in range(h) for j in range(K // 2 if s == 0 else K)]
    n = len(events)
    first, last = (n + 1) // 4, 2 * n // 3
    for e in range(n):
        weights_event(e)
        if e == 0:
            split_hidden()
        if e == min(2, last - 1):
            positions()
        if first <= e < last:
            products((e - first) * n_t // (last - first), (e + 1 - first) * n_t // (last - first))
        if e == last - 1:
            pick(chip(h))
            pick(chip(h - 1))
            pick(chip(1 - h))
        if e >= last:
            sums_event(e - last)

    for k in range(2 * h + 1):
        w_sib(k, 1 - c).wait_recv()
    begin = n - last
    end = max(begin + 1, n - 2)
    for e in range(begin, n):
        sums_event(e)
        if begin <= e < end:
            lo, hi = (e - begin) * n_t // (end - begin), (e + 1 - begin) * n_t // (end - begin)
            if hi == n_t:
                if hi - 1 > lo:
                    lax.fori_loop(1 + lo, n_t, columns_and_send, 0)
                columns(0, 0)
            elif hi > lo:
                lax.fori_loop(1 + lo, 1 + hi, columns_and_send, 0)
        if e == n - 1:
            hidden_gradient()

    proj_acc = psend[t].astype(F32)
    for i in range(1, n_t):
        peer = tpeer(i)
        part_arrival(peer).wait_recv()
        proj_acc += parts[peer].astype(F32)
    proj_ref[...] = proj_acc.astype(BF16)

    def sent_f(i, carry):
        ids_copy(i).wait_send()
        return carry

    def sent_t(i, carry):
        grad_copy(i).wait_send()
        part_copy(tpeer(i)).wait_send()
        return carry

    def sent_g(d, carry):
        g_copy(d).wait_send()
        return carry

    lax.fori_loop(1, n_f, sent_f, 0)
    lax.fori_loop(1, n_t, sent_t, 0)
    lax.fori_loop(0, n_z, sent_g, 0)
    for k in range(2 * h + 1):
        w_sib(k, c).wait_send()
    for s, j in events:
        w_right(s, j).wait_send()
        w_left(s, other(j)).wait_send()
    for s, j in hops:
        right_copy(s, j).wait_send()
        left_copy(s, other(j)).wait_send()

    for j in range(K):
        right_copy(h - 1, j).wait_recv()
        left_copy(h - 1, j).wait_recv()
    grads = g_own[z].astype(F32) + ring_r[h - 1].astype(F32) + ring_l[h - 1].astype(F32)
    flat[...] = grads.reshape(cap * HALF, LANES)
    scale = 1.0 / math.sqrt(toks * n_f)
    for i in range(HALF):
        piece = flat[pl.ds(i, cap, stride=HALF), :]
        gs_ref[0, :, i * LANES:(i + 1) * LANES] = jnp.where(live, piece * scale, 0.0)


def on_device(hidden, grad_out, weight_slots, block_ids, slot_count):
    n_f, n_t = lax.axis_size("fsdp"), lax.axis_size("tensor")
    toks, units = hidden.shape
    cols = grad_out.shape[1]
    cap = weight_slots.shape[1]
    n_z = n_f // 2
    h = n_z // 2
    brows, bcols = units // BLK, n_t * cols // BLK
    block = (cap, HALF, LANES)
    dma = pltpu.SemaphoreType.DMA
    vmem = pl.BlockSpec(memory_space=pltpu.VMEM)
    groups = -(-brows * bcols // LANES)
    projected, d_hidden, grads = pl.pallas_call(
        functools.partial(kernel, n_f, n_t),
        out_shape=(
            pltpu.VMEM((toks, cols), BF16),
            pltpu.VMEM((toks, units), BF16),
            pltpu.VMEM((1, cap, BLK * BLK), F32),
        ),
        in_specs=[vmem] * 4 + [pl.BlockSpec(memory_space=pltpu.SMEM)],
        out_specs=(vmem, vmem, vmem),
        scratch_shapes=[
            pltpu.VMEM((n_f * cap + 8, HALF, LANES), BF16),
            pltpu.VMEM((cap * HALF, LANES), F32),
            pltpu.VMEM(block, BF16),
            pltpu.VMEM((n_f, cap), jnp.int32),
            pltpu.VMEM((n_t, toks, cols), BF16),
            pltpu.VMEM((units // 2, 2 * toks), BF16),
            pltpu.VMEM((2 * toks, units // 2), BF16),
            pltpu.VMEM((2 * n_t, 2 * toks, 2 * LANES), BF16),
            pltpu.VMEM((brows * bcols, HALF, LANES), BF16),
            pltpu.VMEM((2, units // 2, 2 * LANES), BF16),
            pltpu.VMEM((n_z,) + block, BF16),
            pltpu.VMEM((n_z,) + block, BF16),
            pltpu.VMEM((n_z,) + block, BF16),
            pltpu.VMEM((h,) + block, BF16),
            pltpu.VMEM((h,) + block, BF16),
            pltpu.VMEM((h,) + block, BF16),
            pltpu.VMEM((h,) + block, BF16),
            pltpu.VMEM((n_t, toks, cols), BF16),
            pltpu.VMEM((n_t, toks, cols), BF16),
            pltpu.VMEM((2 * toks, units // 2), F32),
            pltpu.VMEM((groups, LANES), jnp.int32),
            pltpu.SMEM((groups, LANES), jnp.int32),
            pltpu.SMEM((n_f, cap), jnp.int32),
            dma((n_f,)), dma((n_f,)), dma((n_t,)), dma((n_t,)),
            dma((h, K)), dma((h, K)), dma((h, K)), dma((h, K)),
            dma((2 * h + 1,)), dma((2 * h + 1,)),
            dma((n_z,)), dma((n_z,)),
            dma((h, K)), dma((h, K)), dma((h, K)), dma((h, K)),
            dma((n_t,)), dma((n_t,)), dma((2,)),
        ],
        compiler_params=pltpu.CompilerParams(
            collective_id=0, has_side_effects=True, vmem_limit_bytes=56 * 1024 * 1024
        ),
        cost_estimate=pl.CostEstimate(
            flops=10 * toks * units * n_t * cols, bytes_accessed=2 * 1024 * 1024, transcendentals=0
        ),
    )(hidden, grad_out, weight_slots, block_ids, slot_count)
    return (projected, d_hidden, grads)


def solution(mesh):
    in_specs = (
        P("fsdp", "tensor"),
        P("fsdp", "tensor"),
        P("tensor", "fsdp", None),
        P("tensor", "fsdp"),
        P("tensor", "fsdp"),
    )
    out_specs = (P("fsdp", "tensor"), P("fsdp", "tensor"), P("tensor", "fsdp", None))
    return jax.shard_map(
        on_device, mesh=mesh, in_specs=in_specs, out_specs=out_specs, check_vma=False
    )
```
